32 devices in a mesh: slab: 8 (over z, y), sub: 4 (over x, core).
Axes of the slice: x: 2, y: 2, z: 4, core: 2. Of those that a mesh axis runs over, the one named last changes fastest.
Arguments:
- right_sides: bfloat16 [65536, 768], P(('slab', 'sub')), may hold values from -6 to 6
- front_sides: bfloat16 [16384, 768], P(('slab', 'sub')), may hold values from -6 to 6
- pending_front: bfloat16 [16384, 256], P(('slab', 'sub')), may hold values from -6 to 6
- inner_index: int32 [512, 6], P(('slab', 'sub')), may hold values from 0 to 15, all different within a row
- inner_blocks: bfloat16 [512, 6, 128, 128], P(('slab', 'sub')), may hold values from -0.15625 to 0.15625
- inner_inverse: bfloat16 [512, 128, 128], P(('slab', 'sub')), may hold values from -1 to 2
- outer_index: int32 [128, 8], P(('slab', 'sub')), may hold values from 0 to 15, all different within a row
- outer_blocks: bfloat16 [128, 8, 128, 128], P(('slab', 'sub')), may hold values from -0.125 to 0.125
- front_inverse: bfloat16 [128, 128, 128], P(('slab', 'sub')), may hold values from -1 to 2
Outputs:
- solution: bfloat16 [65536, 768], P(('slab', 'sub'))
- front_solution: bfloat16 [16384, 768], P(('slab', 'sub'))
The draws below stay inside these ranges and needn't reach their ends.
All inputs are finite; a program needn't handle non-finite values.
Results may differ from the reference program's by a relative error of at most 0.009.
Values may be sent and summed in bfloat16 or wider, within the bound.
No kernel may reach another device: no remote copies, remote signals or barrier semaphores. Data moves between devices by JAX's collectives and lax.ppermute only.
A program may use at most 64 MiB of HBM per device.

```python
import math
import jax
import jax.numpy as jnp
from jax import lax

BLOCK = 128
FRONT = 2048
COLUMNS = 256
TICKS = 3
ROWS_DEV = 2048
FRONT_LINKS = 6
INNER_LINKS = 8
ROWS = 65536
FRONTS = 16384
N_SLAB = 8
N_SUB = 4


def block_inverse(key, block_count):
    random_part = jax.random.truncated_normal(key, -4.0, 4.0, (block_count, BLOCK, BLOCK), jnp.float32)
    matrix = jnp.eye(BLOCK, dtype=jnp.float32)[None] + 0.5 * random_part / math.sqrt(BLOCK)
    return matrix.astype(jnp.bfloat16)


def draw_inner_inverse(key, part):
    return block_inverse(jax.random.fold_in(key, 11), ROWS // BLOCK)


def draw_front_inverse(key, part):
    return block_inverse(jax.random.fold_in(key, 23), FRONTS // BLOCK)


def levels(own_key, extent, split, smallest, top_value):
    def one(axis_at, parts):
        draws = jax.random.uniform(jax.random.fold_in(jax.random.fold_in(own_key, 6), axis_at), (parts,), jnp.float32, smallest / len(split), top_value / len(split))
        return jnp.repeat(jnp.exp(draws), extent[axis_at] // parts).reshape((-1,) + (1,) * (len(extent) - axis_at - 1))

    loudness = one(*split[0])
    for cut in split[1:]:
        loudness = loudness * one(*cut)
    return loudness


def picks_of(stream_key, rows, count, top, lift):
    sequence = jax.random.permutation(jax.random.fold_in(stream_key, 1), count)
    favour = sequence
    for power in range(3):
        favour = favour * favour // count
    favour = favour * lift // count
    tickets = jax.random.randint(jax.random.fold_in(stream_key, 2), (rows, count), 0, 4096) + favour
    sure = jax.random.permutation(jax.random.fold_in(stream_key, 3), rows)[jnp.arange(count) % rows]
    tickets = jnp.where(jnp.arange(rows)[:, None] == sure[None, :], 1 << 14, tickets)
    merit = tickets * count + jnp.arange(count)
    return lax.top_k(merit.astype(jnp.int32), top)[1].astype(jnp.int32)


def normal_values(key, shape, width, reach, pieces=(), kind=jnp.bfloat16):
    factor_of = levels(key, shape, pieces, -0.22, 0.18) if pieces else 1.0
    array = jax.random.normal(key, shape, jnp.float32) * width * factor_of
    return jnp.minimum(jnp.maximum(array, -reach), reach).astype(kind)


def setup_inputs(seed: int = 0) -> dict:
    key_of = jax.random.split(jax.random.key(seed), 10)
    return {
        "right_sides": normal_values(key_of[0], (ROWS, TICKS * COLUMNS), 1.0, 6.0, ((0, 32),)),
        "front_sides": normal_values(key_of[1], (FRONTS, TICKS * COLUMNS), 1.0, 6.0, ((0, 32),)),
        "pending_front": normal_values(key_of[2], (FRONTS, COLUMNS), 1.0, 6.0, ((0, 32),)),
        "inner_index": picks_of(key_of[3], (ROWS // BLOCK), FRONT // BLOCK, FRONT_LINKS, 0),
        "inner_blocks": normal_values(key_of[4], (ROWS // BLOCK, FRONT_LINKS, BLOCK, BLOCK), (2 * FRONT_LINKS * BLOCK) ** -0.5, 0.15625, ((0, 32),)),
        "inner_inverse": draw_inner_inverse(jax.random.fold_in(key_of[9], 71), 0),
        "outer_index": picks_of(key_of[6], (FRONTS // BLOCK), ROWS_DEV // BLOCK, INNER_LINKS, 0),
        "outer_blocks": normal_values(key_of[7], (FRONTS // BLOCK, INNER_LINKS, BLOCK, BLOCK), (2 * INNER_LINKS * BLOCK) ** -0.5, 0.125, ((0, 32),)),
        "front_inverse": draw_front_inverse(jax.random.fold_in(key_of[9], 71), 0),
    }


def slab_group(operands):
    inner_sides, outer_sides, arriving, in_index, in_blocks, in_inverse, out_index, out_blocks, out_inverse = operands
    front_blocks = arriving.reshape(FRONT // BLOCK, BLOCK, COLUMNS)
    picked = front_blocks[in_index]
    coupled = jnp.einsum("qikab,qikbc->qiac", in_blocks.astype(jnp.float32), picked.astype(jnp.float32))
    inner_values = lax.optimization_barrier((inner_sides.astype(jnp.float32) - coupled).astype(jnp.bfloat16))
    solved = jnp.einsum("qiab,qibc->qiac", in_inverse.astype(jnp.float32), inner_values.astype(jnp.float32))
    solved = lax.optimization_barrier(solved.astype(jnp.bfloat16))
    chosen = jax.vmap(lambda values, where: values[where])(solved, out_index)
    outgoing = jnp.einsum("qjkab,qjkbc->qjac", out_blocks.astype(jnp.float32), chosen.astype(jnp.float32))
    outer_values = lax.optimization_barrier((outer_sides.astype(jnp.float32) - outgoing).astype(jnp.bfloat16))
    front_done = jnp.einsum("qjab,qjbc->qjac", out_inverse.astype(jnp.float32), outer_values.astype(jnp.float32))
    return solved, front_done.astype(jnp.bfloat16)


def reference(right_sides, front_sides, pending_front, inner_index, inner_blocks, inner_inverse, outer_index, outer_blocks, front_inverse):
    slabs = N_SLAB
    subs = N_SUB
    inner_rows = ROWS_DEV // BLOCK
    outer_rows = FRONT // (subs * BLOCK)
    sides_all = right_sides.reshape(slabs, subs, inner_rows, BLOCK, TICKS, COLUMNS)
    front_all = front_sides.reshape(slabs, subs, outer_rows, BLOCK, TICKS, COLUMNS)
    in_index = inner_index.reshape(slabs, subs, inner_rows, FRONT_LINKS)
    in_blocks = inner_blocks.reshape(slabs, subs, inner_rows, FRONT_LINKS, BLOCK, BLOCK)
    in_inverse = inner_inverse.reshape(slabs, subs, inner_rows, BLOCK, BLOCK)
    out_index = outer_index.reshape(slabs, subs, outer_rows, INNER_LINKS)
    out_blocks = outer_blocks.reshape(slabs, subs, outer_rows, INNER_LINKS, BLOCK, BLOCK)
    out_inverse = front_inverse.reshape(slabs, subs, outer_rows, BLOCK, BLOCK)
    arriving = pending_front.reshape(slabs, FRONT, COLUMNS)
    solved_list = []
    front_list = []
    for group in range(TICKS):
        solved, front_done = lax.map(slab_group, (sides_all[:, :, :, :, group, :], front_all[:, :, :, :, group, :], arriving, in_index, in_blocks, in_inverse, out_index, out_blocks, out_inverse))
        solved_list.append(solved)
        front_list.append(front_done)
        whole = front_done.reshape(slabs, FRONT, COLUMNS)
        arriving = jnp.concatenate([jnp.zeros((1, FRONT, COLUMNS), jnp.bfloat16), whole[:-1]], axis=0)
    solution = jnp.stack(solved_list, axis=4).reshape(ROWS, TICKS * COLUMNS)
    front_solution = jnp.stack(front_list, axis=4).reshape(FRONTS, TICKS * COLUMNS)
    return solution, front_solution
```

```python
import functools

import jax
import jax.numpy as jnp
from jax import lax
from jax.experimental import pallas as pl
from jax.experimental.pallas import tpu as pltpu
from jax.sharding import PartitionSpec as P

AXES = ("slab", "sub")
VMEM = pltpu.VMEM
MIB = 1 << 20


def permuted(x, slabs, subs, by, flip):
    pairs = [
        (s * subs + q, (s + by) * subs + (q ^ flip))
        for s in range(slabs)
        for q in range(subs)
        if 0 <= s + by < slabs
    ]
    return lax.ppermute(x, AXES, pairs)


def gathered(share, slabs, subs):
    shares = {0: share}
    bit = subs // 2
    while bit:
        for r in list(shares):
            shares[r ^ bit] = permuted(shares[r], slabs, subs, 0, bit)
        bit //= 2
    return [shares[r] for r in range(subs)]


def in_vmem(x):
    return pltpu.with_memory_space_constraint(x, VMEM)


def stage_kernel(count, *refs):
    ins, outs, sems = refs[:count], refs[count : 2 * count], refs[2 * count]
    copies = [
        pltpu.make_async_copy(a, b, sems.at[n])
        for n, (a, b) in enumerate(zip(ins, outs))
    ]
    for c in copies:
        c.start()
    for c in copies:
        c.wait()


def staged(*arrays):
    n = len(arrays)
    size = sum(a.size * a.dtype.itemsize for a in arrays)
    return pl.pallas_call(
        functools.partial(stage_kernel, n),
        out_shape=tuple(VMEM(a.shape, a.dtype) for a in arrays),
        in_specs=[pl.BlockSpec(memory_space=pl.ANY)] * n,
        out_specs=tuple(pl.BlockSpec(memory_space=VMEM) for _ in arrays),
        scratch_shapes=[pltpu.SemaphoreType.DMA((n,))],
        compiler_params=pltpu.CompilerParams(vmem_limit_bytes=2 * MIB),
        cost_estimate=pl.CostEstimate(
            flops=0, bytes_accessed=2 * size, transcendentals=0
        ),
        name="stage",
    )(*[pltpu.with_memory_space_constraint(a, pltpu.HBM) for a in arrays])


def dot(a, b):
    return jnp.dot(a, b, preferred_element_type=jnp.float32)


def part_kernel(subs, width, column, step, aliased, *refs):
    shares, refs = refs[:subs], refs[subs:]
    (in_idx, out_idx, in_blocks, in_inv, out_blocks, out_inv, sides, fronts), refs = (
        refs[:8],
        refs[8:],
    )
    if aliased:
        refs = refs[2:]
    sol_hbm, fsol_hbm, f_ref, inc, sol, sem, fsem = refs
    rows_in, links = in_idx.shape
    rows_out, out_links = out_idx.shape
    size = in_inv.shape[1]
    share = shares[0].shape[0]
    swap = lax.axis_index("sub") * (share // size)
    cols = pl.ds(column * width, width)
    for r, ref in enumerate(shares):
        inc[pl.ds(r * share, share), :] = ref[...]

    def rows_of(ref, block):
        return ref[pl.ds(pl.multiple_of(block * size, size), size), :]

    def out_copy(g):
        rows = pl.ds(pl.multiple_of(g * step * size, size), step * size)
        return pltpu.make_async_copy(
            sol.at[rows, :], sol_hbm.at[rows, cols], sem.at[g]
        )

    def inner(g, _):
        for r in range(step):
            i = g * step + r
            picked = [rows_of(inc, in_idx[i, k] ^ swap) for k in range(links)]
            lhs = jnp.concatenate([in_blocks[i, k] for k in range(links)], axis=1)
            coupled = dot(lhs, jnp.concatenate(picked, axis=0))
            at = pl.ds(pl.multiple_of(i * size, size), size)
            value = (sides[at, cols].astype(jnp.float32) - coupled).astype(jnp.bfloat16)
            sol[at, :] = dot(in_inv[i], value).astype(jnp.bfloat16)
        out_copy(g).start()
        return 0

    lax.fori_loop(0, rows_in // step, inner, 0)
    for j in range(rows_out):
        chosen = [rows_of(sol, out_idx[j, k]) for k in range(out_links)]
        lhs = jnp.concatenate([out_blocks[j, k] for k in range(out_links)], axis=1)
        outgoing = dot(lhs, jnp.concatenate(chosen, axis=0))
        at = pl.ds(j * size, size)
        value = (fronts[at, cols].astype(jnp.float32) - outgoing).astype(jnp.bfloat16)
        f_ref[at, :] = dot(out_inv[j], value).astype(jnp.bfloat16)
    last = pltpu.make_async_copy(f_ref, fsol_hbm.at[:, cols], fsem)
    last.start()
    for g in range(rows_in // step):
        out_copy(g).wait()
    last.wait()


def part(shares, in_idx, out_idx, weights, sides, fronts, outs, column, width):
    subs = len(shares)
    rows, front_rows = sides.shape[0], fronts.shape[0]
    rows_in, links, size, _ = weights[0].shape
    rows_out, out_links = out_idx.shape
    step = next(s for s in (4, 2, 1) if rows_in % s == 0)
    blocks = rows_in * (links + 1) + rows_out * (out_links + 1)
    smem = pl.BlockSpec(memory_space=pltpu.SMEM)
    vmem = pl.BlockSpec(memory_space=VMEM)
    hbm = pl.BlockSpec(memory_space=pl.ANY)
    aliased = outs is not None
    operands = (
        [in_vmem(s) for s in shares]
        + [in_idx, out_idx]
        + [in_vmem(w) for w in weights]
        + [in_vmem(sides), in_vmem(fronts)]
        + (list(outs) if aliased else [])
    )
    n = len(operands)
    return pl.pallas_call(
        functools.partial(part_kernel, subs, width, column, step, aliased),
        out_shape=(
            pltpu.HBM(sides.shape, sides.dtype),
            pltpu.HBM(fronts.shape, fronts.dtype),
            VMEM((front_rows, width), fronts.dtype),
        ),
        in_specs=[vmem] * subs + [smem] * 2 + [vmem] * 6 + [hbm] * (2 * aliased),
        out_specs=(hbm, hbm, vmem),
        scratch_shapes=[
            VMEM((subs * shares[0].shape[0], width), sides.dtype),
            VMEM((rows, width), sides.dtype),
            pltpu.SemaphoreType.DMA((rows_in // step,)),
            pltpu.SemaphoreType.DMA,
        ],
        input_output_aliases={n - 2: 0, n - 1: 1} if aliased else {},
        compiler_params=pltpu.CompilerParams(vmem_limit_bytes=8 * MIB),
        cost_estimate=pl.CostEstimate(
            flops=2 * blocks * size * size * width,
            bytes_accessed=(blocks * size * size + 2 * rows * width) * 2,
            transcendentals=0,
        ),
        name=f"part_{column}",
    )(*operands)


def shards(
    right_sides,
    front_sides,
    pending_front,
    inner_index,
    inner_blocks,
    inner_inverse,
    outer_index,
    outer_blocks,
    front_inverse,
):
    slabs, subs = lax.axis_size("slab"), lax.axis_size("sub")
    columns = pending_front.shape[1]
    groups = right_sides.shape[1] // columns
    halves = 2 if columns % 256 == 0 else 1
    width = columns // halves
    arrived = [
        gathered(pending_front[:, h * width : (h + 1) * width], slabs, subs)
        for h in range(halves)
    ]
    *weights, sides, fronts = staged(
        inner_blocks,
        inner_inverse,
        outer_blocks,
        front_inverse,
        right_sides,
        front_sides,
    )
    outs = None
    for group in range(groups):
        for h in range(halves):
            *outs, front = part(
                arrived[h],
                inner_index,
                outer_index,
                weights,
                sides,
                fronts,
                outs,
                group * halves + h,
                width,
            )
            if group + 1 < groups:
                hop = permuted(front, slabs, subs, 1, 0)
                arrived[h] = gathered(hop, slabs, subs)
    return tuple(outs)


def solution(mesh):
    rows = P(("slab", "sub"), None)
    blocks = P(("slab", "sub"), None, None)
    links = P(("slab", "sub"), None, None, None)
    return jax.shard_map(
        shards,
        mesh=mesh,
        in_specs=(rows, rows, rows, rows, links, blocks, rows, links, blocks),
        out_specs=(rows, rows),
        check_vma=False,
    )
```

```python
import functools

import jax
import jax.numpy as jnp
from jax import lax
from jax.experimental import pallas as pl
from jax.experimental.pallas import tpu as pltpu
from jax.sharding import PartitionSpec as P

AXES = ("slab", "sub")
VMEM = pltpu.VMEM
MIB = 1 << 20


def permuted(x, slabs, subs, by, flip):
    pairs = [
        (s * subs + q, (s + by) * subs + (q ^ flip))
        for s in range(slabs)
        for q in range(subs)
        if 0 <= s + by < slabs
    ]
    return lax.ppermute(x, AXES, pairs)


def gathered(share, slabs, subs):
    shares = {0: share}
    bit = subs // 2
    while bit:
        for r in list(shares):
            shares[r ^ bit] = permuted(shares[r], slabs, subs, 0, bit)
        bit //= 2
    return [shares[r] for r in range(subs)]


def in_vmem(x):
    return pltpu.with_memory_space_constraint(x, VMEM)


def stage_kernel(count, *refs):
    ins, outs, sems = refs[:count], refs[count : 2 * count], refs[2 * count]
    copies = [
        pltpu.make_async_copy(a, b, sems.at[n])
        for n, (a, b) in enumerate(zip(ins, outs))
    ]
    for c in copies:
        c.start()
    for c in copies:
        c.wait()


def staged(*arrays):
    n = len(arrays)
    size = sum(a.size * a.dtype.itemsize for a in arrays)
    return pl.pallas_call(
        functools.partial(stage_kernel, n),
        out_shape=tuple(VMEM(a.shape, a.dtype) for a in arrays),
        in_specs=[pl.BlockSpec(memory_space=pl.ANY)] * n,
        out_specs=tuple(pl.BlockSpec(memory_space=VMEM) for _ in arrays),
        scratch_shapes=[pltpu.SemaphoreType.DMA((n,))],
        compiler_params=pltpu.CompilerParams(vmem_limit_bytes=2 * MIB),
        cost_estimate=pl.CostEstimate(
            flops=0, bytes_accessed=2 * size, transcendentals=0
        ),
        name="stage",
    )(*[pltpu.with_memory_space_constraint(a, pltpu.HBM) for a in arrays])


def dot(a, b):
    return jnp.dot(a, b, preferred_element_type=jnp.float32)


def part_kernel(subs, width, column, aliased, *refs):
    shares, refs = refs[:subs], refs[subs:]
    (in_idx, out_idx, in_blocks, in_inv, out_blocks, out_inv, sides, fronts), refs = (
        refs[:8],
        refs[8:],
    )
    if aliased:
        refs = refs[2:]
    sol_hbm, fsol_hbm, f_ref, inc, val, sol, sem, fsem = refs
    rows_in, links = in_idx.shape
    rows_out, out_links = out_idx.shape
    size = in_inv.shape[1]
    share = shares[0].shape[0]
    swap = lax.axis_index("sub") * (share // size)
    cols = pl.ds(column * width, width)
    for r, ref in enumerate(shares):
        inc[pl.ds(r * share, share), :] = ref[...]

    def rows_of(ref, block):
        return ref[pl.ds(pl.multiple_of(block * size, size), size), :]

    def at(i):
        return pl.ds(i * size, size)

    def side(ref, i):
        return ref[at(i), cols].astype(jnp.float32)

    def row_of(ref, index, i, source, count, flip):
        lhs = jnp.concatenate([ref[i, k] for k in range(count)], axis=1)
        blocks = [rows_of(source, index[i, k] ^ flip) for k in range(count)]
        return dot(lhs, jnp.concatenate(blocks, axis=0))

    for i in range(rows_in):
        coupled = row_of(in_blocks, in_idx, i, inc, links, swap)
        val[at(i), :] = (side(sides, i) - coupled).astype(val.dtype)
    for i in range(rows_in):
        sol[at(i), :] = dot(in_inv[i], val[at(i), :]).astype(sol.dtype)
    first = pltpu.make_async_copy(sol, sol_hbm.at[:, cols], sem)
    first.start()
    for j in range(rows_out):
        outgoing = row_of(out_blocks, out_idx, j, sol, out_links, 0)
        val[at(j), :] = (side(fronts, j) - outgoing).astype(val.dtype)
    for j in range(rows_out):
        f_ref[at(j), :] = dot(out_inv[j], val[at(j), :]).astype(f_ref.dtype)
    last = pltpu.make_async_copy(f_ref, fsol_hbm.at[:, cols], fsem)
    last.start()
    first.wait()
    last.wait()


def part(shares, in_idx, out_idx, weights, sides, fronts, outs, column, width):
    subs = len(shares)
    rows, front_rows = sides.shape[0], fronts.shape[0]
    rows_in, links, size, _ = weights[0].shape
    rows_out, out_links = out_idx.shape
    blocks = rows_in * (links + 1) + rows_out * (out_links + 1)
    smem = pl.BlockSpec(memory_space=pltpu.SMEM)
    vmem = pl.BlockSpec(memory_space=VMEM)
    hbm = pl.BlockSpec(memory_space=pl.ANY)
    aliased = outs is not None
    operands = (
        [in_vmem(s) for s in shares]
        + [in_idx, out_idx]
        + [in_vmem(w) for w in weights]
        + [in_vmem(sides), in_vmem(fronts)]
        + (list(outs) if aliased else [])
    )
    n = len(operands)
    return pl.pallas_call(
        functools.partial(part_kernel, subs, width, column, aliased),
        out_shape=(
            pltpu.HBM(sides.shape, sides.dtype),
            pltpu.HBM(fronts.shape, fronts.dtype),
            VMEM((front_rows, width), fronts.dtype),
        ),
        in_specs=[vmem] * subs + [smem] * 2 + [vmem] * 6 + [hbm] * (2 * aliased),
        out_specs=(hbm, hbm, vmem),
        scratch_shapes=[
            VMEM((subs * shares[0].shape[0], width), sides.dtype),
            VMEM((rows, width), sides.dtype),
            VMEM((rows, width), sides.dtype),
            pltpu.SemaphoreType.DMA,
            pltpu.SemaphoreType.DMA,
        ],
        input_output_aliases={n - 2: 0, n - 1: 1} if aliased else {},
        compiler_params=pltpu.CompilerParams(vmem_limit_bytes=8 * MIB),
        cost_estimate=pl.CostEstimate(
            flops=2 * blocks * size * size * width,
            bytes_accessed=(blocks * size * size + 2 * rows * width) * 2,
            transcendentals=0,
        ),
        name=f"part_{column}",
    )(*operands)


def shards(
    right_sides,
    front_sides,
    pending_front,
    inner_index,
    inner_blocks,
    inner_inverse,
    outer_index,
    outer_blocks,
    front_inverse,
):
    slabs, subs = lax.axis_size("slab"), lax.axis_size("sub")
    columns = pending_front.shape[1]
    groups = right_sides.shape[1] // columns
    halves = 2 if columns % 256 == 0 else 1
    width = columns // halves
    arrived = [
        gathered(pending_front[:, h * width : (h + 1) * width], slabs, subs)
        for h in range(halves)
    ]
    *weights, sides, fronts = staged(
        inner_blocks,
        inner_inverse,
        outer_blocks,
        front_inverse,
        right_sides,
        front_sides,
    )
    outs = None
    for group in range(groups):
        for h in range(halves):
            *outs, front = part(
                arrived[h],
                inner_index,
                outer_index,
                weights,
                sides,
                fronts,
                outs,
                group * halves + h,
                width,
            )
            if group + 1 < groups:
                hop = permuted(front, slabs, subs, 1, 0)
                arrived[h] = gathered(hop, slabs, subs)
    return tuple(outs)


def solution(mesh):
    rows = P(("slab", "sub"), None)
    blocks = P(("slab", "sub"), None, None)
    links = P(("slab", "sub"), None, None, None)
    return jax.shard_map(
        shards,
        mesh=mesh,
        in_specs=(rows, rows, rows, rows, links, blocks, rows, links, blocks),
        out_specs=(rows, rows),
        check_vma=False,
    )
```

```python
import functools

import jax
import jax.numpy as jnp
from jax import lax
from jax.experimental import pallas as pl
from jax.experimental.pallas import tpu as pltpu
from jax.sharding import PartitionSpec as P

AXES = ("slab", "sub")
VMEM = pltpu.VMEM
SCOPED = 16 << 20


def permuted(x, slabs, subs, by, flip, ring=False):
    pairs = [
        (s * subs + q, (s + by) % slabs * subs + (q ^ flip))
        for s in range(slabs)
        for q in range(subs)
        if ring or 0 <= s + by < slabs
    ]
    return lax.ppermute(x, AXES, pairs)


def gathered(share, slabs, subs, before=None):
    shares = {0: share}
    bit = subs // 2
    while bit:
        new = {r ^ bit: permuted(shares[r], slabs, subs, 0, bit) for r in shares}
        if before is not None and bit == 2:
            new, before = lax.optimization_barrier((new, before))
        shares.update(new)
        bit //= 2
    return [shares[r] for r in range(subs)], before


def stage_kernel(counts, *refs):
    ins, outs, (token, sems) = (
        refs[: sum(counts)],
        refs[sum(counts) : -2],
        refs[-2:],
    )
    copies, n = [], 0
    for out, count in zip(outs, counts):
        row = 0
        for _ in range(count):
            at = pl.ds(row, ins[n].shape[0])
            copies.append(pltpu.make_async_copy(ins[n], out.at[at, :], sems.at[n]))
            row += ins[n].shape[0]
            n += 1
    for c in copies:
        c.start()
    token[...] = jnp.zeros_like(token)
    for c in copies:
        c.wait()


def staged(*lists):
    counts = [len(arrays) for arrays in lists]
    flat = [a for arrays in lists for a in arrays]
    size = sum(a.size * a.dtype.itemsize for a in flat)
    rows = [sum(a.shape[0] for a in arrays) for arrays in lists]
    n = len(flat)
    return pl.pallas_call(
        functools.partial(stage_kernel, counts),
        out_shape=(
            *(VMEM((r, a[0].shape[1]), a[0].dtype) for r, a in zip(rows, lists)),
            VMEM((8, 128), jnp.float32),
        ),
        in_specs=[pl.BlockSpec(memory_space=pl.ANY)] * n,
        out_specs=(pl.BlockSpec(memory_space=VMEM),) * (len(lists) + 1),
        scratch_shapes=[pltpu.SemaphoreType.DMA((n,))],
        compiler_params=pltpu.CompilerParams(vmem_limit_bytes=SCOPED),
        cost_estimate=pl.CostEstimate(
            flops=0, bytes_accessed=2 * size, transcendentals=0
        ),
        name="stage",
    )(*[pltpu.with_memory_space_constraint(a, pltpu.HBM) for a in flat])


def dot(a, b):
    return jnp.dot(a, b, preferred_element_type=jnp.float32)


def group_kernel(subs, group, masked, *refs):
    shares, (in_idx, out_idx, blocks, sides) = refs[:subs], refs[subs : subs + 4]
    sol_hbm, fsol_hbm, f_ref, inc, val, sol, sem, fsem = refs[-8:]
    links, rows_in = in_idx.shape
    rows_out, out_links = out_idx.shape
    size = blocks.shape[1]
    share, width = shares[0].shape
    inv_at = rows_in * links
    out_at = inv_at + rows_in
    last_at = out_at + rows_out * out_links
    swap = lax.axis_index("sub") * (share // size)
    cols = pl.ds(group * width, width)
    keep = lax.axis_index("slab") > 0
    for r, ref in enumerate(shares):
        value = ref[...]
        if masked:
            value = jnp.where(keep, value, jnp.zeros_like(value))
        inc[pl.ds(r * share, share), :] = value

    def at(i):
        return pl.ds(i * size, size)

    def side(i):
        return sides[at(i), cols].astype(jnp.float32)

    def block(i):
        return blocks[at(i), :]

    def picked(ref, block):
        return ref[pl.ds(pl.multiple_of(block * size, size), size), :]

    def row_of(first, i, source, places):
        n = len(places)
        lhs = [block(first + i * n + k) for k in range(n)]
        rhs = [picked(source, p) for p in places]
        return dot(jnp.concatenate(lhs, axis=1), jnp.concatenate(rhs, axis=0))

    for i in range(rows_in):
        coupled = row_of(0, i, inc, [in_idx[k, i] ^ swap for k in range(links)])
        val[at(i), :] = (side(i) - coupled).astype(val.dtype)
    for i in range(rows_in):
        sol[at(i), :] = dot(block(inv_at + i), val[at(i), :]).astype(sol.dtype)
    first = pltpu.make_async_copy(sol, sol_hbm.at[:, cols], sem)
    first.start()
    for j in range(rows_out):
        outgoing = row_of(out_at, j, sol, [out_idx[j, k] for k in range(out_links)])
        val[at(j), :] = (side(rows_in + j) - outgoing).astype(val.dtype)
    for j in range(rows_out):
        f_ref[at(j), :] = dot(block(last_at + j), val[at(j), :]).astype(f_ref.dtype)
    last = pltpu.make_async_copy(f_ref, fsol_hbm.at[:, cols], fsem)
    last.start()
    first.wait()
    last.wait()


def group_of(shares, in_idx, out_idx, blocks, sides, outs, token, group, masked):
    subs = len(shares)
    share, width = shares[0].shape
    links, rows_in = in_idx.shape
    rows_out, out_links = out_idx.shape
    size = blocks.shape[1]
    rows, front_rows = rows_in * size, rows_out * size
    count = rows_in * (links + 1) + rows_out * (out_links + 1)
    smem = pl.BlockSpec(memory_space=pltpu.SMEM)
    vmem = pl.BlockSpec(memory_space=VMEM)
    hbm = pl.BlockSpec(memory_space=pl.ANY)
    aliased = outs is not None

    def held(arrays):
        return [pltpu.with_memory_space_constraint(a, VMEM) for a in arrays]

    operands = (
        held(shares)
        + [in_idx, out_idx]
        + held([blocks, sides])
        + (list(outs) if aliased else [])
        + ([] if token is None else [token])
    )
    n = len(operands) - (token is not None)
    return pl.pallas_call(
        functools.partial(group_kernel, subs, group, masked),
        out_shape=(
            pltpu.HBM((rows, sides.shape[1]), sides.dtype),
            pltpu.HBM((front_rows, sides.shape[1]), sides.dtype),
            VMEM((front_rows, width), sides.dtype),
        ),
        in_specs=[vmem] * subs + [smem] * 2 + [vmem] * 2
        + [hbm] * (len(operands) - subs - 4),
        out_specs=(hbm, hbm, vmem),
        scratch_shapes=[
            VMEM((subs * share, width), sides.dtype),
            VMEM((rows, width), sides.dtype),
            VMEM((rows, width), sides.dtype),
            pltpu.SemaphoreType.DMA,
            pltpu.SemaphoreType.DMA,
        ],
        input_output_aliases={n - 2: 0, n - 1: 1} if aliased else {},
        compiler_params=pltpu.CompilerParams(vmem_limit_bytes=SCOPED),
        cost_estimate=pl.CostEstimate(
            flops=2 * count * size * size * width,
            bytes_accessed=(count * size * size + 2 * rows * width) * 2,
            transcendentals=0,
        ),
        name=f"group_{group}",
    )(*operands)


def shards(
    right_sides,
    front_sides,
    pending_front,
    inner_index,
    inner_blocks,
    inner_inverse,
    outer_index,
    outer_blocks,
    front_inverse,
):
    slabs, subs = lax.axis_size("slab"), lax.axis_size("sub")
    columns = pending_front.shape[1]
    groups = right_sides.shape[1] // columns
    in_idx, out_idx = inner_index.T, outer_index
    size = inner_inverse.shape[1]
    weights = (inner_blocks, inner_inverse, outer_blocks, front_inverse)
    blocks, sides, token = staged(
        [w.reshape(-1, size) for w in weights], [right_sides, front_sides]
    )
    arrived, token = gathered(pending_front, slabs, subs, token)
    outs = None
    for group in range(groups):
        ring = group + 2 < groups
        *outs, front = group_of(
            arrived,
            in_idx,
            out_idx,
            blocks,
            sides,
            outs,
            token,
            group,
            0 < group and group + 1 < groups,
        )
        if group + 1 < groups:
            hop = permuted(front, slabs, subs, 1, 0, ring)
            arrived, token = gathered(hop, slabs, subs)
    return tuple(outs)


def solution(mesh):
    rows = P(("slab", "sub"), None)
    blocks = P(("slab", "sub"), None, None)
    links = P(("slab", "sub"), None, None, None)
    return jax.shard_map(
        shards,
        mesh=mesh,
        in_specs=(rows, rows, rows, rows, links, blocks, rows, links, blocks),
        out_specs=(rows, rows),
        check_vma=False,
    )
```

```python
import functools

import jax
import jax.numpy as jnp
from jax import lax
from jax.experimental import pallas as pl
from jax.experimental.pallas import tpu as pltpu
from jax.sharding import PartitionSpec as P

AXES = ("slab", "sub")
VMEM = pltpu.VMEM
SCOPED = 16 << 20


def permuted(x, slabs, subs, by, flip, ring=False):
    pairs = [
        (s * subs + q, (s + by) % slabs * subs + (q ^ flip))
        for s in range(slabs)
        for q in range(subs)
        if ring or 0 <= s + by < slabs
    ]
    return lax.ppermute(x, AXES, pairs)


def gathered(share, slabs, subs, before=None):
    shares = {0: share}
    bit = subs // 2
    while bit:
        new = {r ^ bit: permuted(shares[r], slabs, subs, 0, bit) for r in shares}
        if before is not None and bit == 2:
            new, before = lax.optimization_barrier((new, before))
        shares.update(new)
        bit //= 2
    return [shares[r] for r in range(subs)], before


def stage_kernel(counts, *refs):
    ins, outs, (token, sems) = (
        refs[: sum(counts)],
        refs[sum(counts) : -2],
        refs[-2:],
    )
    copies, n = [], 0
    for out, count in zip(outs, counts):
        row = 0
        for _ in range(count):
            at = pl.ds(row, ins[n].shape[0])
            copies.append(pltpu.make_async_copy(ins[n], out.at[at, :], sems.at[n]))
            row += ins[n].shape[0]
            n += 1
    for c in copies:
        c.start()
    token[...] = jnp.zeros_like(token)
    for c in copies:
        c.wait()


def staged(*lists):
    counts = [len(arrays) for arrays in lists]
    flat = [a for arrays in lists for a in arrays]
    size = sum(a.size * a.dtype.itemsize for a in flat)
    rows = [sum(a.shape[0] for a in arrays) for arrays in lists]
    n = len(flat)
    return pl.pallas_call(
        functools.partial(stage_kernel, counts),
        out_shape=(
            *(VMEM((r, a[0].shape[1]), a[0].dtype) for r, a in zip(rows, lists)),
            VMEM((8, 128), jnp.float32),
        ),
        in_specs=[pl.BlockSpec(memory_space=pl.ANY)] * n,
        out_specs=(pl.BlockSpec(memory_space=VMEM),) * (len(lists) + 1),
        scratch_shapes=[pltpu.SemaphoreType.DMA((n,))],
        compiler_params=pltpu.CompilerParams(vmem_limit_bytes=SCOPED),
        cost_estimate=pl.CostEstimate(
            flops=0, bytes_accessed=2 * size, transcendentals=0
        ),
        name="stage",
    )(*[pltpu.with_memory_space_constraint(a, pltpu.HBM) for a in flat])


def dot(a, b):
    return jnp.dot(a, b, preferred_element_type=jnp.float32)


def group_kernel(count, group, masked, chunks, *refs):
    shares, (in_idx, out_idx, blocks, sides) = refs[:count], refs[count : count + 4]
    (sol_hbm, fsol_hbm), (inc, val, sol, sem, fsem) = (
        refs[-7 - chunks : -5 - chunks],
        refs[-5:],
    )
    f_refs = refs[-5 - chunks : -5]
    links, rows_in = in_idx.shape
    rows_out, out_links = out_idx.shape
    size = blocks.shape[1]
    part, width = shares[0].shape
    inv_at = rows_in * links
    out_at = inv_at + rows_in
    last_at = out_at + rows_out * out_links
    swap = lax.axis_index("sub") * rows_out
    cols = pl.ds(group * width, width)
    keep = lax.axis_index("slab") > 0
    for r, ref in enumerate(shares):
        value = ref[...]
        if masked:
            value = jnp.where(keep, value, jnp.zeros_like(value))
        inc[pl.ds(r * part, part), :] = value

    def at(i):
        return pl.ds(i * size, size)

    def side(i):
        return sides[at(i), cols].astype(jnp.float32)

    def block(i):
        return blocks[at(i), :]

    def picked(ref, block):
        return ref[pl.ds(pl.multiple_of(block * size, size), size), :]

    def row_of(first, i, source, places):
        n = len(places)
        lhs = [block(first + i * n + k) for k in range(n)]
        rhs = [picked(source, p) for p in places]
        return dot(jnp.concatenate(lhs, axis=1), jnp.concatenate(rhs, axis=0))

    for i in range(rows_in):
        coupled = row_of(0, i, inc, [in_idx[k, i] ^ swap for k in range(links)])
        val[at(i), :] = (side(i) - coupled).astype(val.dtype)
    for i in range(rows_in):
        sol[at(i), :] = dot(block(inv_at + i), val[at(i), :]).astype(sol.dtype)
    first = pltpu.make_async_copy(sol, sol_hbm.at[:, cols], sem)
    first.start()
    for j in range(rows_out):
        outgoing = row_of(out_at, j, sol, [out_idx[j, k] for k in range(out_links)])
        val[at(j), :] = (side(rows_in + j) - outgoing).astype(val.dtype)
    each = rows_out // chunks
    copies = [first]
    for c, f_ref in enumerate(f_refs):
        for j in range(each):
            row = c * each + j
            f_ref[at(j), :] = dot(block(last_at + row), val[at(row), :]).astype(
                f_ref.dtype
            )
        there = fsol_hbm.at[pl.ds(c * each * size, each * size), cols]
        copies.append(pltpu.make_async_copy(f_ref, there, fsem.at[c]))
        copies[-1].start()
    for c in copies:
        c.wait()


def group_of(shares, in_idx, out_idx, blocks, sides, outs, token, group, masked):
    width = shares[0].shape[1]
    links, rows_in = in_idx.shape
    rows_out, out_links = out_idx.shape
    size = blocks.shape[1]
    rows, front_rows = rows_in * size, rows_out * size
    chunks = 2 if rows_out % 2 == 0 else 1
    pieces = len(shares)
    count = rows_in * (links + 1) + rows_out * (out_links + 1)
    smem = pl.BlockSpec(memory_space=pltpu.SMEM)
    vmem = pl.BlockSpec(memory_space=VMEM)
    hbm = pl.BlockSpec(memory_space=pl.ANY)
    aliased = outs is not None

    def held(arrays):
        return [pltpu.with_memory_space_constraint(a, VMEM) for a in arrays]

    operands = (
        held(shares)
        + [in_idx, out_idx]
        + held([blocks, sides])
        + (list(outs) if aliased else [])
        + ([] if token is None else [token])
    )
    n = len(operands) - (token is not None)
    return pl.pallas_call(
        functools.partial(group_kernel, pieces, group, masked, chunks),
        out_shape=(
            pltpu.HBM((rows, sides.shape[1]), sides.dtype),
            pltpu.HBM((front_rows, sides.shape[1]), sides.dtype),
            *[VMEM((front_rows // chunks, width), sides.dtype)] * chunks,
        ),
        in_specs=[vmem] * pieces + [smem] * 2 + [vmem] * 2
        + [hbm] * (len(operands) - pieces - 4),
        out_specs=(hbm, hbm, *[vmem] * chunks),
        scratch_shapes=[
            VMEM((sum(a.shape[0] for a in shares), width), sides.dtype),
            VMEM((rows, width), sides.dtype),
            VMEM((rows, width), sides.dtype),
            pltpu.SemaphoreType.DMA,
            pltpu.SemaphoreType.DMA((chunks,)),
        ],
        input_output_aliases={n - 2: 0, n - 1: 1} if aliased else {},
        compiler_params=pltpu.CompilerParams(vmem_limit_bytes=SCOPED),
        cost_estimate=pl.CostEstimate(
            flops=2 * count * size * size * width,
            bytes_accessed=(count * size * size + 2 * rows * width) * 2,
            transcendentals=0,
        ),
        name=f"group_{group}",
    )(*operands)


def shards(
    right_sides,
    front_sides,
    pending_front,
    inner_index,
    inner_blocks,
    inner_inverse,
    outer_index,
    outer_blocks,
    front_inverse,
):
    slabs, subs = lax.axis_size("slab"), lax.axis_size("sub")
    columns = pending_front.shape[1]
    groups = right_sides.shape[1] // columns
    in_idx, out_idx = inner_index.T, outer_index
    size = inner_inverse.shape[1]
    weights = (inner_blocks, inner_inverse, outer_blocks, front_inverse)
    blocks, sides, token = staged(
        [w.reshape(-1, size) for w in weights], [right_sides, front_sides]
    )
    arrived, token = gathered(pending_front, slabs, subs, token)
    outs = None
    for group in range(groups):
        ring = group + 2 < groups
        made = group_of(
            arrived,
            in_idx,
            out_idx,
            blocks,
            sides,
            outs,
            token,
            group,
            0 < group and group + 1 < groups,
        )
        outs, fronts = made[:2], made[2:]
        if group + 1 < groups:
            hops = [permuted(f, slabs, subs, 1, 0, ring) for f in fronts]
            chunks, token = [gathered(hop, slabs, subs)[0] for hop in hops], None
            arrived = [c[r] for r in range(subs) for c in chunks]
    return tuple(outs)


def solution(mesh):
    rows = P(("slab", "sub"), None)
    blocks = P(("slab", "sub"), None, None)
    links = P(("slab", "sub"), None, None, None)
    return jax.shard_map(
        shards,
        mesh=mesh,
        in_specs=(rows, rows, rows, rows, links, blocks, rows, links, blocks),
        out_specs=(rows, rows),
        check_vma=False,
    )
```

```python
import functools

import jax
import jax.numpy as jnp
from jax import lax
from jax.experimental import pallas as pl
from jax.experimental.pallas import tpu as pltpu
from jax.sharding import PartitionSpec as P

AXES = ("slab", "sub")
VMEM = pltpu.VMEM
SCOPED = 16 << 20
PARTS = 1


def permuted(x, slabs, subs, by, flip, ring=False):
    pairs = [
        (s * subs + q, (s + by) % slabs * subs + (q ^ flip))
        for s in range(slabs)
        for q in range(subs)
        if ring or 0 <= s + by < slabs
    ]
    return lax.ppermute(x, AXES, pairs)


def gathered(share, slabs, subs, before=None):
    shares = {0: share}
    bit = subs // 2
    while bit:
        new = {r ^ bit: permuted(shares[r], slabs, subs, 0, bit) for r in shares}
        if before is not None and bit == 2:
            new, before = lax.optimization_barrier((new, before))
        shares.update(new)
        bit //= 2
    return [shares[r] for r in range(subs)], before


def stage_kernel(counts, *refs):
    ins, outs, (token, sems) = (
        refs[: sum(counts)],
        refs[sum(counts) : -2],
        refs[-2:],
    )
    copies, n = [], 0
    for out, count in zip(outs, counts):
        row = 0
        for _ in range(count):
            at = pl.ds(row, ins[n].shape[0])
            copies.append(pltpu.make_async_copy(ins[n], out.at[at, :], sems.at[n]))
            row += ins[n].shape[0]
            n += 1
    for c in copies:
        c.start()
    token[...] = jnp.zeros_like(token)
    for c in copies:
        c.wait()


def staged(*lists):
    counts = [len(arrays) for arrays in lists]
    flat = [a for arrays in lists for a in arrays]
    size = sum(a.size * a.dtype.itemsize for a in flat)
    rows = [sum(a.shape[0] for a in arrays) for arrays in lists]
    n = len(flat)
    return pl.pallas_call(
        functools.partial(stage_kernel, counts),
        out_shape=(
            *(VMEM((r, a[0].shape[1]), a[0].dtype) for r, a in zip(rows, lists)),
            VMEM((8, 128), jnp.float32),
        ),
        in_specs=[pl.BlockSpec(memory_space=pl.ANY)] * n,
        out_specs=(pl.BlockSpec(memory_space=VMEM),) * (len(lists) + 1),
        scratch_shapes=[pltpu.SemaphoreType.DMA((n,))],
        compiler_params=pltpu.CompilerParams(vmem_limit_bytes=SCOPED),
        cost_estimate=pl.CostEstimate(
            flops=0, bytes_accessed=2 * size, transcendentals=0
        ),
        name="stage",
    )(*[pltpu.with_memory_space_constraint(a, pltpu.HBM) for a in flat])


def dot(a, b):
    return jnp.dot(a, b, preferred_element_type=jnp.float32)


def group_kernel(count, group, groups, masked, chunks, *refs):
    shares, (in_idx, out_idx, blocks, sides) = refs[:count], refs[count : count + 4]
    refs = refs[count + 4 :]
    done = group + 1 == groups
    if done:
        sol_hbm, fsol_hbm, sol, *f_refs, inc, val, sems = refs[-6 - chunks :]
    else:
        sol, *f_refs, inc, val = refs[-3 - chunks :]
    links, rows_in = in_idx.shape
    rows_out, out_links = out_idx.shape
    size = blocks.shape[1]
    part, width = shares[0].shape
    each = rows_out // chunks
    inv_at = rows_in * links
    out_at = inv_at + rows_in
    last_at = out_at + rows_out * out_links
    swap = lax.axis_index("sub") * rows_out
    cols = pl.ds(group * width, width)
    copies = []

    def write(source, target, first, count):
        there = target.at[pl.ds(first, count), cols]
        copies.append(pltpu.make_async_copy(source, there, sems.at[len(copies)]))
        copies[-1].start()

    keep = lax.axis_index("slab") > 0
    for r, ref in enumerate(shares):
        value = ref[...]
        if masked:
            value = jnp.where(keep, value, jnp.zeros_like(value))
        inc[pl.ds(r * part, part), :] = value

    def at(i):
        return pl.ds(i * size, size)

    def side(i):
        return sides[at(i), cols].astype(jnp.float32)

    def block(i):
        return blocks[at(i), :]

    def picked(ref, block):
        return ref[pl.ds(pl.multiple_of(block * size, size), size), :]

    def row_of(first, i, source, places):
        n = len(places)
        lhs = [block(first + i * n + k) for k in range(n)]
        rhs = [picked(source, p) for p in places]
        return dot(jnp.concatenate(lhs, axis=1), jnp.concatenate(rhs, axis=0))

    for i in range(rows_in):
        coupled = row_of(0, i, inc, [in_idx[k, i] ^ swap for k in range(links)])
        val[at(i), :] = (side(i) - coupled).astype(val.dtype)
    some = rows_in // PARTS
    for i in range(rows_in):
        sol[at(i), :] = dot(block(inv_at + i), val[at(i), :]).astype(sol.dtype)
        if done and (i + 1) % some == 0:
            start, count = (i + 1 - some) * size, some * size
            piece = sol.at[pl.ds(start, count), :]
            write(piece, sol_hbm, start, count)
    for j in range(rows_out):
        outgoing = row_of(out_at, j, sol, [out_idx[j, k] for k in range(out_links)])
        val[at(j), :] = (side(rows_in + j) - outgoing).astype(val.dtype)
    for c, f_ref in enumerate(f_refs):
        for j in range(each):
            row = c * each + j
            f_ref[at(j), :] = dot(block(last_at + row), val[at(row), :]).astype(
                f_ref.dtype
            )
        if done:
            count = each * size
            write(f_ref, fsol_hbm, c * count, count)
    for c in copies:
        c.wait()


def group_of(shares, in_idx, out_idx, blocks, sides, outs, token, group, groups, masked):
    width = shares[0].shape[1]
    links, rows_in = in_idx.shape
    rows_out, out_links = out_idx.shape
    size, dtype = blocks.shape[1], blocks.dtype
    rows, front_rows = rows_in * size, rows_out * size
    chunks = 2 if rows_out % 2 == 0 else 1
    pieces = len(shares)
    count = rows_in * (links + 1) + rows_out * (out_links + 1)
    smem = pl.BlockSpec(memory_space=pltpu.SMEM)
    vmem = pl.BlockSpec(memory_space=VMEM)
    hbm = pl.BlockSpec(memory_space=pl.ANY)
    done = group + 1 == groups

    def held(arrays):
        return [pltpu.with_memory_space_constraint(a, VMEM) for a in arrays]

    operands = held(shares) + [in_idx, out_idx] + held([blocks, sides])
    in_specs = [vmem] * pieces + [smem] * 2 + [vmem] * 2
    aliases = {len(operands) + n: n for n in range(len(outs))}
    operands += [*outs] if token is None else [*outs, token]
    in_specs += [hbm] * (len(operands) - len(in_specs))
    own = [VMEM((rows, width), dtype)]
    own += [VMEM((front_rows // chunks, width), dtype)] * chunks
    out_shape, out_specs = own, [vmem] * len(own)
    scratch = [
        VMEM((sum(a.shape[0] for a in shares), width), dtype),
        VMEM((rows, width), dtype),
    ]
    if done:
        wide = sides.shape[1]
        scratch = own + scratch + [pltpu.SemaphoreType.DMA((PARTS + chunks,))]
        out_shape = [pltpu.HBM((r, wide), dtype) for r in (rows, front_rows)]
        out_specs = [hbm, hbm]
    return pl.pallas_call(
        functools.partial(group_kernel, pieces, group, groups, masked, chunks),
        out_shape=tuple(out_shape),
        in_specs=in_specs,
        out_specs=tuple(out_specs),
        scratch_shapes=scratch,
        input_output_aliases=aliases,
        compiler_params=pltpu.CompilerParams(vmem_limit_bytes=SCOPED),
        cost_estimate=pl.CostEstimate(
            flops=2 * count * size * size * width,
            bytes_accessed=(count * size * size + 2 * rows * width) * 2,
            transcendentals=0,
        ),
        name=f"group_{group}",
    )(*operands)


def flush_kernel(count, column, *refs):
    sources, (sol_hbm, fsol_hbm, sems) = refs[:count], refs[-3:]
    copies, row = [], 0
    for n, ref in enumerate(sources):
        rows, width = ref.shape
        out = fsol_hbm if n else sol_hbm
        there = out.at[pl.ds(row, rows), pl.ds(column * width, width)]
        row += rows if n else 0
        copies.append(pltpu.make_async_copy(ref, there, sems.at[n]))
        copies[-1].start()
    for c in copies:
        c.wait()


def flushed(sources, outs, column, groups):
    n, dtype = len(sources), sources[0].dtype
    wide = groups * sources[0].shape[1]
    rows = (sources[0].shape[0], sum(f.shape[0] for f in sources[1:]))
    hbm = pl.BlockSpec(memory_space=pl.ANY)
    return pl.pallas_call(
        functools.partial(flush_kernel, n, column),
        out_shape=tuple(pltpu.HBM((r, wide), dtype) for r in rows),
        in_specs=[pl.BlockSpec(memory_space=VMEM)] * n + [hbm] * len(outs),
        out_specs=(hbm, hbm),
        scratch_shapes=[pltpu.SemaphoreType.DMA((n,))],
        input_output_aliases={n + k: k for k in range(len(outs))},
        compiler_params=pltpu.CompilerParams(vmem_limit_bytes=SCOPED),
        cost_estimate=pl.CostEstimate(
            flops=0,
            bytes_accessed=2 * sum(s.size for s in sources) * dtype.itemsize,
            transcendentals=0,
        ),
        name=f"flush_{column}",
    )(*[pltpu.with_memory_space_constraint(s, VMEM) for s in sources], *outs)


def shards(
    right_sides,
    front_sides,
    pending_front,
    inner_index,
    inner_blocks,
    inner_inverse,
    outer_index,
    outer_blocks,
    front_inverse,
):
    slabs, subs = lax.axis_size("slab"), lax.axis_size("sub")
    columns = pending_front.shape[1]
    groups = right_sides.shape[1] // columns
    in_idx, out_idx = inner_index.T, outer_index
    size = inner_inverse.shape[1]
    weights = (inner_blocks, inner_inverse, outer_blocks, front_inverse)
    blocks, sides, token = staged(
        [w.reshape(-1, size) for w in weights], [right_sides, front_sides]
    )
    arrived, token = gathered(pending_front, slabs, subs, token)
    outs = ()
    for group in range(groups):
        made = group_of(
            arrived,
            in_idx,
            out_idx,
            blocks,
            sides,
            outs if group + 1 == groups else (),
            token if group == 0 else None,
            group,
            groups,
            0 < group and group + 1 < groups,
        )
        if group + 1 < groups:
            ring = group + 2 < groups
            hops = [permuted(f, slabs, subs, 1, 0, ring) for f in made[1:]]
            outs = flushed(made, outs, group, groups)
            chunks = []
            for n, hop in enumerate(hops):
                chunk, ahead = gathered(hop, slabs, subs, None if n else outs)
                outs = outs if n else ahead
                chunks.append(chunk)
            arrived = [c[r] for r in range(subs) for c in chunks]
    return tuple(made[:2])


def solution(mesh):
    rows = P(("slab", "sub"), None)
    blocks = P(("slab", "sub"), None, None)
    links = P(("slab", "sub"), None, None, None)
    return jax.shard_map(
        shards,
        mesh=mesh,
        in_specs=(rows, rows, rows, rows, links, blocks, rows, links, blocks),
        out_specs=(rows, rows),
        check_vma=False,
    )
```

```python
import functools

import jax
import jax.numpy as jnp
from jax import lax
from jax.experimental import pallas as pl
from jax.experimental.pallas import tpu as pltpu
from jax.sharding import PartitionSpec as P

AXES = ("slab", "sub")
VMEM = pltpu.VMEM
SCOPED = 16 << 20
PARTS = 1


def permuted(x, slabs, subs, by, flip, ring=False):
    pairs = [
        (s * subs + q, (s + by) % slabs * subs + (q ^ flip))
        for s in range(slabs)
        for q in range(subs)
        if ring or 0 <= s + by < slabs
    ]
    return lax.ppermute(x, AXES, pairs)


def gathered(share, slabs, subs, before=None):
    shares = {0: share}
    bit = subs // 2
    while bit:
        new = {r ^ bit: permuted(shares[r], slabs, subs, 0, bit) for r in shares}
        if before is not None and bit == 2:
            new, before = lax.optimization_barrier((new, before))
        shares.update(new)
        bit //= 2
    return [shares[r] for r in range(subs)], before


def stage_kernel(counts, *refs):
    ins, outs, (token, sems) = (
        refs[: sum(counts)],
        refs[sum(counts) : -2],
        refs[-2:],
    )
    copies, n = [], 0
    for out, count in zip(outs, counts):
        row = 0
        for _ in range(count):
            at = pl.ds(row, ins[n].shape[0])
            copies.append(pltpu.make_async_copy(ins[n], out.at[at, :], sems.at[n]))
            row += ins[n].shape[0]
            n += 1
    for c in copies:
        c.start()
    token[...] = jnp.zeros_like(token)
    for c in copies:
        c.wait()


def staged(*lists):
    counts = [len(arrays) for arrays in lists]
    flat = [a for arrays in lists for a in arrays]
    size = sum(a.size * a.dtype.itemsize for a in flat)
    rows = [sum(a.shape[0] for a in arrays) for arrays in lists]
    n = len(flat)
    return pl.pallas_call(
        functools.partial(stage_kernel, counts),
        out_shape=(
            *(VMEM((r, a[0].shape[1]), a[0].dtype) for r, a in zip(rows, lists)),
            VMEM((8, 128), jnp.float32),
        ),
        in_specs=[pl.BlockSpec(memory_space=pl.ANY)] * n,
        out_specs=(pl.BlockSpec(memory_space=VMEM),) * (len(lists) + 1),
        scratch_shapes=[pltpu.SemaphoreType.DMA((n,))],
        compiler_params=pltpu.CompilerParams(vmem_limit_bytes=SCOPED),
        cost_estimate=pl.CostEstimate(
            flops=0, bytes_accessed=2 * size, transcendentals=0
        ),
        name="stage",
    )(*[pltpu.with_memory_space_constraint(a, pltpu.HBM) for a in flat])


def dot(a, b):
    return jnp.dot(a, b, preferred_element_type=jnp.float32)


def rows_of(ref, i, size):
    return ref[pl.ds(i * size, size), :]


def row_sum(blocks, first, i, source, places):
    size, n = blocks.shape[1], len(places)
    lhs = [rows_of(blocks, first + i * n + k, size) for k in range(n)]
    rhs = [source[pl.ds(pl.multiple_of(p * size, size), size), :] for p in places]
    return dot(jnp.concatenate(lhs, axis=1), jnp.concatenate(rhs, axis=0))


def finish(blocks, first, out_idx, sides, cols, val, sol, f_refs, write):
    rows_out, out_links = out_idx.shape
    size = blocks.shape[1]
    rows_in = val.shape[0] // size
    out_at = first + rows_in
    last_at = out_at + rows_out * out_links
    some, each = rows_in // PARTS, rows_out // len(f_refs)
    where = out_idx[...]
    for i in range(rows_in):
        at = pl.ds(i * size, size)
        sol[at, :] = dot(rows_of(blocks, first + i, size), val[at, :]).astype(sol.dtype)
        if write and (i + 1) % some == 0:
            start, count = (i + 1 - some) * size, some * size
            write(sol.at[pl.ds(start, count), :], 0, start, count)
    for j in range(rows_out):
        at = pl.ds(j * size, size)
        places = [where[j, k] for k in range(out_links)]
        outgoing = row_sum(blocks, out_at, j, sol, places)
        side = sides[pl.ds((rows_in + j) * size, size), cols].astype(jnp.float32)
        val[at, :] = (side - outgoing).astype(val.dtype)
    for c, f_ref in enumerate(f_refs):
        for j in range(each):
            row = c * each + j
            value = dot(rows_of(blocks, last_at + row, size), rows_of(val, row, size))
            f_ref[pl.ds(j * size, size), :] = value.astype(f_ref.dtype)
        if write:
            write(f_ref, 1, c * each * size, each * size)


def writer(targets, cols, sems):
    copies = []

    def write(source, target, first, count):
        there = targets[target].at[pl.ds(first, count), cols]
        copies.append(pltpu.make_async_copy(source, there, sems.at[len(copies)]))
        copies[-1].start()

    return write, copies


def group_kernel(pieces, group, groups, chunks, *refs):
    shares, (in_idx, out_idx, blocks, sides) = refs[:pieces], refs[pieces : pieces + 4]
    done = group + 1 == groups
    if done:
        sol_hbm, fsol_hbm, sol, *f_refs, inc, val, sems = refs[-6 - chunks :]
    else:
        sol, *f_refs, inc, val = refs[-3 - chunks :]
    links, rows_in = in_idx.shape
    size = blocks.shape[1]
    part, width = shares[0].shape
    cols = pl.ds(group * width, width)
    swap = lax.axis_index("sub") * out_idx.shape[0]
    behind = lax.axis_index("slab") > 0

    def couple():
        for r, ref in enumerate(shares):
            inc[pl.ds(r * part, part), :] = ref[...]
        where = in_idx[...] ^ swap
        for i in range(rows_in):
            at = pl.ds(i * size, size)
            places = [where[k, i] for k in range(links)]
            coupled = row_sum(blocks, 0, i, inc, places)
            value = sides[at, cols].astype(jnp.float32) - coupled
            val[at, :] = value.astype(val.dtype)

    def rest(write=None):
        finish(
            blocks, rows_in * links, out_idx, sides, cols, val, sol, f_refs, write
        )

    if done:

        def whole():
            couple()
            write, copies = writer((sol_hbm, fsol_hbm), cols, sems)
            rest(write)
            for c in copies:
                c.wait()

        if group == 0:
            whole()
        else:
            pl.when(behind)(whole)
        return
    if group == 0:
        couple()
    else:
        pl.when(behind)(couple)

        @pl.when(jnp.logical_not(behind))
        def _():
            val[...] = sides[pl.ds(0, rows_in * size), cols]

    rest()


def group_of(shares, in_idx, out_idx, blocks, sides, outs, token, group, groups):
    width = shares[0].shape[1]
    links, rows_in = in_idx.shape
    rows_out, out_links = out_idx.shape
    size, dtype = blocks.shape[1], blocks.dtype
    rows, front_rows = rows_in * size, rows_out * size
    chunks = 2 if rows_out % 2 == 0 else 1
    pieces = len(shares)
    count = rows_in * (links + 1) + rows_out * (out_links + 1)
    vmem = pl.BlockSpec(memory_space=VMEM)
    hbm = pl.BlockSpec(memory_space=pl.ANY)
    done = group + 1 == groups

    def held(arrays):
        return [pltpu.with_memory_space_constraint(a, VMEM) for a in arrays]

    operands = held([*shares, in_idx, out_idx, blocks, sides])
    in_specs = [vmem] * len(operands)
    aliases = {len(operands) + n: n for n in range(len(outs))}
    operands += [*outs] if token is None else [*outs, token]
    in_specs += [hbm] * (len(operands) - len(in_specs))
    own = [VMEM((rows, width), dtype)]
    own += [VMEM((front_rows // chunks, width), dtype)] * chunks
    out_shape, out_specs = own, [vmem] * len(own)
    scratch = [
        VMEM((sum(a.shape[0] for a in shares), width), dtype),
        VMEM((rows, width), dtype),
    ]
    if done:
        wide = sides.shape[1]
        scratch = own + scratch + [pltpu.SemaphoreType.DMA((PARTS + chunks,))]
        out_shape = [pltpu.HBM((r, wide), dtype) for r in (rows, front_rows)]
        out_specs = [hbm, hbm]
    return pl.pallas_call(
        functools.partial(group_kernel, pieces, group, groups, chunks),
        out_shape=tuple(out_shape),
        in_specs=in_specs,
        out_specs=tuple(out_specs),
        scratch_shapes=scratch,
        input_output_aliases=aliases,
        compiler_params=pltpu.CompilerParams(vmem_limit_bytes=SCOPED),
        cost_estimate=pl.CostEstimate(
            flops=2 * count * size * size * width,
            bytes_accessed=(count * size * size + 2 * rows * width) * 2,
            transcendentals=0,
        ),
        name=f"group_{group}",
    )(*operands)


def flush_kernel(count, column, ahead, *refs):
    sources = refs[:count]
    width = sources[0].shape[1]
    if ahead:
        out_idx, blocks, sides = refs[count : count + 3]
        *outs, val, sol = refs[-5 - count : -1 - count]
        *f_refs, more, sems = refs[-1 - count :]
    else:
        *outs, sems = refs[-3:]
    write, copies = writer(outs, pl.ds(column * width, width), sems)
    row = 0
    for n, ref in enumerate(sources):
        rows = ref.shape[0]
        write(ref, min(n, 1), row, rows)
        row += rows if n else 0
    if ahead:

        @pl.when(lax.axis_index("slab") == 0)
        def _():
            cols = pl.ds((column + 1) * width, width)
            to, made = writer(outs, cols, more)
            val[...] = sides[pl.ds(0, val.shape[0]), cols]
            size = blocks.shape[1]
            rows_out, links = out_idx.shape
            later = val.shape[0] // size + rows_out * (links + 1)
            first = blocks.shape[0] // size - later
            finish(blocks, first, out_idx, sides, cols, val, sol, f_refs, to)
            for c in made:
                c.wait()

    for c in copies:
        c.wait()


def flushed(sources, out_idx, blocks, sides, outs, column, groups):
    n, dtype = len(sources), sources[0].dtype
    wide = sides.shape[1]
    rows = (sources[0].shape[0], sum(f.shape[0] for f in sources[1:]))
    hbm = pl.BlockSpec(memory_space=pl.ANY)
    vmem = pl.BlockSpec(memory_space=VMEM)
    ahead = column + 2 == groups
    ins = [*sources, out_idx, blocks, sides] if ahead else [*sources]
    held = [pltpu.with_memory_space_constraint(a, VMEM) for a in ins]
    own = [VMEM(sources[0].shape, dtype), *[VMEM(a.shape, dtype) for a in sources]]
    own.append(pltpu.SemaphoreType.DMA((PARTS + n - 1,)))
    return pl.pallas_call(
        functools.partial(flush_kernel, n, column, ahead),
        out_shape=tuple(pltpu.HBM((r, wide), dtype) for r in rows),
        in_specs=[vmem] * len(ins) + [hbm] * len(outs),
        out_specs=(hbm, hbm),
        scratch_shapes=own * ahead + [pltpu.SemaphoreType.DMA((n,))],
        input_output_aliases={len(ins) + k: k for k in range(len(outs))},
        compiler_params=pltpu.CompilerParams(vmem_limit_bytes=SCOPED),
        cost_estimate=pl.CostEstimate(
            flops=0,
            bytes_accessed=2 * sum(a.size for a in sources) * dtype.itemsize,
            transcendentals=0,
        ),
        name=f"flush_{column}",
    )(*held, *outs)


def shards(
    right_sides,
    front_sides,
    pending_front,
    inner_index,
    inner_blocks,
    inner_inverse,
    outer_index,
    outer_blocks,
    front_inverse,
):
    slabs, subs = lax.axis_size("slab"), lax.axis_size("sub")
    columns = pending_front.shape[1]
    groups = right_sides.shape[1] // columns
    in_idx, out_idx = inner_index.T, outer_index
    size = inner_inverse.shape[1]
    weights = (inner_blocks, inner_inverse, outer_blocks, front_inverse)
    blocks, sides, token = staged(
        [w.reshape(-1, size) for w in weights], [right_sides, front_sides]
    )
    arrived, token = gathered(pending_front, slabs, subs, token)
    outs = ()
    for group in range(groups):
        made = group_of(
            arrived,
            in_idx,
            out_idx,
            blocks,
            sides,
            outs if group + 1 == groups else (),
            token if group == 0 else None,
            group,
            groups,
        )
        if group + 1 < groups:
            ring = True
            hops = [permuted(f, slabs, subs, 1, 0, ring) for f in made[1:]]
            outs = flushed(made, out_idx, blocks, sides, outs, group, groups)
            chunks = []
            for n, hop in enumerate(hops):
                chunk, ahead = gathered(hop, slabs, subs, None if n else outs)
                outs = outs if n else ahead
                chunks.append(chunk)
            arrived = [c[r] for r in range(subs) for c in chunks]
    return tuple(made[:2])


def solution(mesh):
    rows = P(("slab", "sub"), None)
    blocks = P(("slab", "sub"), None, None)
    links = P(("slab", "sub"), None, None, None)
    return jax.shard_map(
        shards,
        mesh=mesh,
        in_specs=(rows, rows, rows, rows, links, blocks, rows, links, blocks),
        out_specs=(rows, rows),
        check_vma=False,
    )
```

```python
import functools

import jax
import jax.numpy as jnp
from jax import lax
from jax.experimental import pallas as pl
from jax.experimental.pallas import tpu as pltpu
from jax.sharding import PartitionSpec as P

AXES = ("slab", "sub")
VMEM = pltpu.VMEM
SCOPED = 16 << 20
PARTS = 2
LAG = 8


def permuted(x, slabs, subs, by, flip, ring=False):
    pairs = [
        (s * subs + q, (s + by) % slabs * subs + (q ^ flip))
        for s in range(slabs)
        for q in range(subs)
        if ring or 0 <= s + by < slabs
    ]
    return lax.ppermute(x, AXES, pairs)


def gathered(share, slabs, subs, before=None):
    shares = {0: share}
    bit = subs // 2
    while bit:
        new = {r ^ bit: permuted(shares[r], slabs, subs, 0, bit) for r in shares}
        if before is not None and bit == 2:
            new, before = lax.optimization_barrier((new, before))
        shares.update(new)
        bit //= 2
    return [shares[r] for r in range(subs)], before


def stage_kernel(counts, *refs):
    ins, outs, (token, sems) = (
        refs[: sum(counts)],
        refs[sum(counts) : -2],
        refs[-2:],
    )
    copies, n = [], 0
    for out, count in zip(outs, counts):
        row = 0
        for _ in range(count):
            at = pl.ds(row, ins[n].shape[0])
            copies.append(pltpu.make_async_copy(ins[n], out.at[at, :], sems.at[n]))
            row += ins[n].shape[0]
            n += 1
    for c in copies:
        c.start()
    token[...] = jnp.zeros_like(token)
    for c in copies:
        c.wait()


def staged(*lists):
    counts = [len(arrays) for arrays in lists]
    flat = [a for arrays in lists for a in arrays]
    size = sum(a.size * a.dtype.itemsize for a in flat)
    rows = [sum(a.shape[0] for a in arrays) for arrays in lists]
    n = len(flat)
    return pl.pallas_call(
        functools.partial(stage_kernel, counts),
        out_shape=(
            *(VMEM((r, a[0].shape[1]), a[0].dtype) for r, a in zip(rows, lists)),
            VMEM((8, 128), jnp.float32),
        ),
        in_specs=[pl.BlockSpec(memory_space=pl.ANY)] * n,
        out_specs=(pl.BlockSpec(memory_space=VMEM),) * (len(lists) + 1),
        scratch_shapes=[pltpu.SemaphoreType.DMA((n,))],
        compiler_params=pltpu.CompilerParams(vmem_limit_bytes=SCOPED),
        cost_estimate=pl.CostEstimate(
            flops=0, bytes_accessed=2 * size, transcendentals=0
        ),
        name="stage",
    )(*[pltpu.with_memory_space_constraint(a, pltpu.HBM) for a in flat])


def dot(a, b):
    return jnp.dot(a, b, preferred_element_type=jnp.float32)


def rows_of(ref, i, size):
    return ref[pl.ds(i * size, size), :]


def row_sum(blocks, first, i, source, places):
    size, n = blocks.shape[1], len(places)
    lhs = [rows_of(blocks, first + i * n + k, size) for k in range(n)]
    rhs = [source[pl.ds(pl.multiple_of(p * size, size), size), :] for p in places]
    return dot(jnp.concatenate(lhs, axis=1), jnp.concatenate(rhs, axis=0))


def solve(inner, blocks, first, out_idx, sides, cols, val, sol, f_refs, write=None):
    rows_out, out_links = out_idx.shape
    size = blocks.shape[1]
    rows_in = val.shape[0] // size
    out_at = first + rows_in
    last_at = out_at + rows_out * out_links
    some, each = rows_in // PARTS, rows_out // len(f_refs)
    where = out_idx[...]
    lag = min(LAG, rows_in)
    for ahead in range(rows_in + lag):
        if ahead < rows_in:
            val[pl.ds(ahead * size, size), :] = inner(ahead).astype(val.dtype)
        i = ahead - lag
        if i < 0:
            continue
        at = pl.ds(i * size, size)
        sol[at, :] = dot(rows_of(blocks, first + i, size), val[at, :]).astype(sol.dtype)
        if write and (i + 1) % some == 0:
            start, count = (i + 1 - some) * size, some * size
            write(sol.at[pl.ds(start, count), :], 0, start, count)
    for j in range(rows_out):
        at = pl.ds(j * size, size)
        places = [where[j, k] for k in range(out_links)]
        outgoing = row_sum(blocks, out_at, j, sol, places)
        side = sides[pl.ds((rows_in + j) * size, size), cols].astype(jnp.float32)
        val[at, :] = (side - outgoing).astype(val.dtype)
    for c, f_ref in enumerate(f_refs):
        for j in range(each):
            row = c * each + j
            value = dot(rows_of(blocks, last_at + row, size), rows_of(val, row, size))
            f_ref[pl.ds(j * size, size), :] = value.astype(f_ref.dtype)
        if write:
            write(f_ref, 1, c * each * size, each * size)


def writer(targets, cols, sems):
    copies = []

    def write(source, target, first, count):
        there = targets[target].at[pl.ds(first, count), cols]
        copies.append(pltpu.make_async_copy(source, there, sems.at[len(copies)]))
        copies[-1].start()

    return write, copies


def group_kernel(pieces, group, groups, chunks, *refs):
    shares, (in_idx, out_idx, blocks, sides) = refs[:pieces], refs[pieces : pieces + 4]
    done = group + 1 == groups
    if done:
        sol_hbm, fsol_hbm, sol, *f_refs, inc, val, sems = refs[-6 - chunks :]
    else:
        sol, *f_refs, inc, val = refs[-3 - chunks :]
    links, rows_in = in_idx.shape
    size = blocks.shape[1]
    part, width = shares[0].shape
    cols = pl.ds(group * width, width)
    swap = lax.axis_index("sub") * out_idx.shape[0]
    behind = lax.axis_index("slab") > 0

    def side(i):
        return sides[pl.ds(i * size, size), cols]

    def whole():
        for r, ref in enumerate(shares):
            inc[pl.ds(r * part, part), :] = ref[...]
        where = in_idx[...] ^ swap

        def inner(i):
            places = [where[k, i] for k in range(links)]
            coupled = row_sum(blocks, 0, i, inc, places)
            return side(i).astype(jnp.float32) - coupled

        if not done:
            rest(inner)
            return
        write, copies = writer((sol_hbm, fsol_hbm), cols, sems)
        rest(inner, write)
        for c in copies:
            c.wait()

    def rest(inner, write=None):
        first = rows_in * links
        solve(inner, blocks, first, out_idx, sides, cols, val, sol, f_refs, write)

    if group == 0:
        whole()
        return
    pl.when(behind)(whole)


def group_of(shares, in_idx, out_idx, blocks, sides, given, token, group, groups):
    width = shares[0].shape[1]
    links, rows_in = in_idx.shape
    rows_out, out_links = out_idx.shape
    size, dtype = blocks.shape[1], blocks.dtype
    rows, front_rows = rows_in * size, rows_out * size
    chunks = 2 if rows_out % 2 == 0 else 1
    pieces = len(shares)
    count = rows_in * (links + 1) + rows_out * (out_links + 1)
    vmem = pl.BlockSpec(memory_space=VMEM)
    hbm = pl.BlockSpec(memory_space=pl.ANY)
    done = group + 1 == groups

    def held(arrays):
        return [pltpu.with_memory_space_constraint(a, VMEM) for a in arrays]

    operands = held([*shares, in_idx, out_idx, blocks, sides])
    in_specs = [vmem] * len(operands)
    aliases = {len(operands) + n: n for n in range(len(given))}
    if done:
        operands += [*given]
        in_specs += [hbm] * len(given)
    else:
        operands += held(given)
        in_specs += [vmem] * len(given)
    if token is not None:
        operands.append(token)
        in_specs.append(hbm)
    own = [VMEM((rows, width), dtype)]
    own += [VMEM((front_rows // chunks, width), dtype)] * chunks
    out_shape, out_specs = own, [vmem] * len(own)
    scratch = [
        VMEM((sum(a.shape[0] for a in shares), width), dtype),
        VMEM((rows, width), dtype),
    ]
    if done:
        wide = sides.shape[1]
        scratch = own + scratch + [pltpu.SemaphoreType.DMA((PARTS + chunks,))]
        out_shape = [pltpu.HBM((r, wide), dtype) for r in (rows, front_rows)]
        out_specs = [hbm, hbm]
    return pl.pallas_call(
        functools.partial(group_kernel, pieces, group, groups, chunks),
        out_shape=tuple(out_shape),
        in_specs=in_specs,
        out_specs=tuple(out_specs),
        scratch_shapes=scratch,
        input_output_aliases=aliases,
        compiler_params=pltpu.CompilerParams(vmem_limit_bytes=SCOPED),
        cost_estimate=pl.CostEstimate(
            flops=2 * count * size * size * width,
            bytes_accessed=(count * size * size + 2 * rows * width) * 2,
            transcendentals=0,
        ),
        name=f"group_{group}",
    )(*operands)


def flush_kernel(count, column, groups, *refs):
    sources, (out_idx, blocks, sides) = refs[:count], refs[count : count + 3]
    width = sources[0].shape[1]
    last = column + 2 == groups
    if last:
        sol_hbm, fsol_hbm, sol, *f_refs, val, more, sems = refs[-5 - count :]
    else:
        sol_hbm, fsol_hbm, sol, *f_refs, val, sems = refs[-4 - count :]
    outs = (sol_hbm, fsol_hbm)
    write, copies = writer(outs, pl.ds(column * width, width), sems)
    row = 0
    for n, ref in enumerate(sources):
        rows = ref.shape[0]
        write(ref, min(n, 1), row, rows)
        row += rows if n else 0

    @pl.when(lax.axis_index("slab") == 0)
    def _():
        cols = pl.ds((column + 1) * width, width)
        to, made = writer(outs, cols, more) if last else (None, [])
        size = blocks.shape[1]
        rows_out, links = out_idx.shape
        later = val.shape[0] // size + rows_out * (links + 1)
        first = blocks.shape[0] // size - later

        def inner(i):
            return sides[pl.ds(i * size, size), cols]

        solve(inner, blocks, first, out_idx, sides, cols, val, sol, f_refs, to)
        for c in made:
            c.wait()

    for c in copies:
        c.wait()


def flushed(sources, out_idx, blocks, sides, outs, column, groups):
    n, dtype = len(sources), sources[0].dtype
    wide = sides.shape[1]
    rows = (sources[0].shape[0], sum(f.shape[0] for f in sources[1:]))
    hbm = pl.BlockSpec(memory_space=pl.ANY)
    vmem = pl.BlockSpec(memory_space=VMEM)
    ins = [*sources, out_idx, blocks, sides]
    held = [pltpu.with_memory_space_constraint(a, VMEM) for a in ins]
    own = [VMEM(a.shape, dtype) for a in sources]
    out_shape = [pltpu.HBM((r, wide), dtype) for r in rows]
    out_specs = [hbm, hbm]
    scratch = [VMEM(sources[0].shape, dtype)]
    if column + 2 == groups:
        scratch = own + scratch + [pltpu.SemaphoreType.DMA((PARTS + n - 1,))]
    else:
        out_shape, out_specs = out_shape + own, out_specs + [vmem] * n
    made = pl.pallas_call(
        functools.partial(flush_kernel, n, column, groups),
        out_shape=tuple(out_shape),
        in_specs=[vmem] * len(ins) + [hbm] * len(outs),
        out_specs=tuple(out_specs),
        scratch_shapes=scratch + [pltpu.SemaphoreType.DMA((n,))],
        input_output_aliases={len(ins) + k: k for k in range(len(outs))},
        compiler_params=pltpu.CompilerParams(vmem_limit_bytes=SCOPED),
        cost_estimate=pl.CostEstimate(
            flops=0,
            bytes_accessed=2 * sum(a.size for a in sources) * dtype.itemsize,
            transcendentals=0,
        ),
        name=f"flush_{column}",
    )(*held, *outs)
    return made[:2], made[2:]


def shards(
    right_sides,
    front_sides,
    pending_front,
    inner_index,
    inner_blocks,
    inner_inverse,
    outer_index,
    outer_blocks,
    front_inverse,
):
    slabs, subs = lax.axis_size("slab"), lax.axis_size("sub")
    columns = pending_front.shape[1]
    groups = right_sides.shape[1] // columns
    in_idx, out_idx = inner_index.T, outer_index
    size = inner_inverse.shape[1]
    weights = (inner_blocks, inner_inverse, outer_blocks, front_inverse)
    blocks, sides, token = staged(
        [w.reshape(-1, size) for w in weights], [right_sides, front_sides]
    )
    arrived, token = gathered(pending_front, slabs, subs, token)
    outs = early = ()
    for group in range(groups):
        made = group_of(
            arrived,
            in_idx,
            out_idx,
            blocks,
            sides,
            outs if group + 1 == groups else early,
            token if group == 0 else None,
            group,
            groups,
        )
        if group + 1 < groups:
            ring = True
            hops = [permuted(f, slabs, subs, 1, 0, ring) for f in made[1:]]
            outs, early = flushed(made, out_idx, blocks, sides, outs, group, groups)
            chunks = []
            for n, hop in enumerate(hops):
                chunk, ahead = gathered(hop, slabs, subs, None if n else outs)
                outs = outs if n else ahead
                chunks.append(chunk)
            arrived = [c[r] for r in range(subs) for c in chunks]
    return tuple(made[:2])


def solution(mesh):
    rows = P(("slab", "sub"), None)
    blocks = P(("slab", "sub"), None, None)
    links = P(("slab", "sub"), None, None, None)
    return jax.shard_map(
        shards,
        mesh=mesh,
        in_specs=(rows, rows, rows, rows, links, blocks, rows, links, blocks),
        out_specs=(rows, rows),
        check_vma=False,
    )
```

```python
import functools

import jax
import jax.numpy as jnp
from jax import lax
from jax.experimental import pallas as pl
from jax.experimental.pallas import tpu as pltpu
from jax.sharding import PartitionSpec as P

AXES = ("slab", "sub")
VMEM = pltpu.VMEM
SCOPED = 16 << 20
PARTS = 2
LAG = 8


def permuted(x, slabs, subs, by, flip, ring=False):
    pairs = [
        (s * subs + q, (s + by) % slabs * subs + (q ^ flip))
        for s in range(slabs)
        for q in range(subs)
        if ring or 0 <= s + by < slabs
    ]
    return lax.ppermute(x, AXES, pairs)


def gathered(share, slabs, subs, before=None):
    shares = {0: share}
    bit = subs // 2
    while bit:
        new = {r ^ bit: permuted(shares[r], slabs, subs, 0, bit) for r in shares}
        if before is not None and bit == 2:
            new, before = lax.optimization_barrier((new, before))
        shares.update(new)
        bit //= 2
    return [shares[r] for r in range(subs)], before


def stage_kernel(counts, *refs):
    ins, outs, (token, sems) = (
        refs[: sum(counts)],
        refs[sum(counts) : -2],
        refs[-2:],
    )
    copies, n = [], 0
    for out, count in zip(outs, counts):
        row = 0
        for _ in range(count):
            at = pl.ds(row, ins[n].shape[0])
            copies.append(pltpu.make_async_copy(ins[n], out.at[at, :], sems.at[n]))
            row += ins[n].shape[0]
            n += 1
    for c in copies:
        c.start()
    token[...] = jnp.zeros_like(token)
    for c in copies:
        c.wait()


def staged(*lists):
    counts = [len(arrays) for arrays in lists]
    flat = [a for arrays in lists for a in arrays]
    size = sum(a.size * a.dtype.itemsize for a in flat)
    rows = [sum(a.shape[0] for a in arrays) for arrays in lists]
    n = len(flat)
    return pl.pallas_call(
        functools.partial(stage_kernel, counts),
        out_shape=(
            *(VMEM((r, a[0].shape[1]), a[0].dtype) for r, a in zip(rows, lists)),
            VMEM((8, 128), jnp.float32),
        ),
        in_specs=[pl.BlockSpec(memory_space=pl.ANY)] * n,
        out_specs=(pl.BlockSpec(memory_space=VMEM),) * (len(lists) + 1),
        scratch_shapes=[pltpu.SemaphoreType.DMA((n,))],
        compiler_params=pltpu.CompilerParams(vmem_limit_bytes=SCOPED),
        cost_estimate=pl.CostEstimate(
            flops=0, bytes_accessed=2 * size, transcendentals=0
        ),
        name="stage",
    )(*[pltpu.with_memory_space_constraint(a, pltpu.HBM) for a in flat])


def dot(a, b):
    return jnp.dot(a, b, preferred_element_type=jnp.float32)


def rows_of(ref, i, size):
    return ref[pl.ds(i * size, size), :]


def row_sum(blocks, first, i, source, places):
    size, n = blocks.shape[1], len(places)
    lhs = [rows_of(blocks, first + i * n + k, size) for k in range(n)]
    rhs = [source[pl.ds(pl.multiple_of(p * size, size), size), :] for p in places]
    return dot(jnp.concatenate(lhs, axis=1), jnp.concatenate(rhs, axis=0))


def solve(inner, blocks, first, out_idx, sides, cols, val, sol, f_refs, write=None):
    rows_out, out_links = out_idx.shape
    size = blocks.shape[1]
    rows_in = val.shape[0] // size
    out_at = first + rows_in
    last_at = out_at + rows_out * out_links
    some, each = rows_in // PARTS, rows_out // len(f_refs)
    where = out_idx[...]
    lag = min(LAG, rows_in)
    for ahead in range(rows_in + lag):
        if ahead < rows_in:
            val[pl.ds(ahead * size, size), :] = inner(ahead).astype(val.dtype)
        i = ahead - lag
        if i < 0:
            continue
        at = pl.ds(i * size, size)
        sol[at, :] = dot(rows_of(blocks, first + i, size), val[at, :]).astype(sol.dtype)
        if write and (i + 1) % some == 0:
            start, count = (i + 1 - some) * size, some * size
            write(sol.at[pl.ds(start, count), :], 0, start, count)
    for j in range(rows_out):
        at = pl.ds(j * size, size)
        places = [where[j, k] for k in range(out_links)]
        outgoing = row_sum(blocks, out_at, j, sol, places)
        side = sides[pl.ds((rows_in + j) * size, size), cols].astype(jnp.float32)
        val[at, :] = (side - outgoing).astype(val.dtype)
    for c, f_ref in enumerate(f_refs):
        for j in range(each):
            row = c * each + j
            value = dot(rows_of(blocks, last_at + row, size), rows_of(val, row, size))
            f_ref[pl.ds(j * size, size), :] = value.astype(f_ref.dtype)
        if write:
            write(f_ref, 1, c * each * size, each * size)


def writer(targets, cols, sems):
    copies = []

    def write(source, target, first, count):
        there = targets[target].at[pl.ds(first, count), cols]
        copies.append(pltpu.make_async_copy(source, there, sems.at[len(copies)]))
        copies[-1].start()

    return write, copies


def group_kernel(pieces, group, groups, chunks, *refs):
    shares, (in_idx, out_idx, blocks, sides) = refs[:pieces], refs[pieces : pieces + 4]
    done = group + 1 == groups
    if done:
        sol_hbm, fsol_hbm, sol, *f_refs, inc, val, sems = refs[-6 - chunks :]
    else:
        sol, *f_refs, inc, val = refs[-3 - chunks :]
    links, rows_in = in_idx.shape
    size = blocks.shape[1]
    part, width = shares[0].shape
    cols = pl.ds(group * width, width)
    swap = lax.axis_index("sub") * out_idx.shape[0]
    behind = lax.axis_index("slab") > 0

    def side(i):
        return sides[pl.ds(i * size, size), cols]

    def whole():
        for r, ref in enumerate(shares):
            inc[pl.ds(r * part, part), :] = ref[...]
        where = in_idx[...] ^ swap

        def inner(i):
            places = [where[k, i] for k in range(links)]
            coupled = row_sum(blocks, 0, i, inc, places)
            return side(i).astype(jnp.float32) - coupled

        if not done:
            rest(inner)
            return
        write, copies = writer((sol_hbm, fsol_hbm), cols, sems)
        rest(inner, write)
        for c in copies:
            c.wait()

    def rest(inner, write=None):
        first = rows_in * links
        solve(inner, blocks, first, out_idx, sides, cols, val, sol, f_refs, write)

    if group == 0:
        whole()
        return
    pl.when(behind)(whole)


def group_of(shares, in_idx, out_idx, blocks, sides, given, token, group, groups):
    width = shares[0].shape[1]
    links, rows_in = in_idx.shape
    rows_out, out_links = out_idx.shape
    size, dtype = blocks.shape[1], blocks.dtype
    rows, front_rows = rows_in * size, rows_out * size
    chunks = 2 if rows_out % 2 == 0 else 1
    pieces = len(shares)
    count = rows_in * (links + 1) + rows_out * (out_links + 1)
    vmem = pl.BlockSpec(memory_space=VMEM)
    hbm = pl.BlockSpec(memory_space=pl.ANY)
    done = group + 1 == groups

    def held(arrays):
        return [pltpu.with_memory_space_constraint(a, VMEM) for a in arrays]

    operands = held([*shares, in_idx, out_idx, blocks, sides])
    in_specs = [vmem] * len(operands)
    aliases = {len(operands) + n: n for n in range(len(given))}
    if done:
        operands += [*given]
        in_specs += [hbm] * len(given)
    else:
        operands += held(given)
        in_specs += [vmem] * len(given)
    if token is not None:
        operands.append(token)
        in_specs.append(hbm)
    own = [VMEM((rows, width), dtype)]
    own += [VMEM((front_rows // chunks, width), dtype)] * chunks
    out_shape, out_specs = own, [vmem] * len(own)
    scratch = [
        VMEM((sum(a.shape[0] for a in shares), width), dtype),
        VMEM((rows, width), dtype),
    ]
    if done:
        wide = sides.shape[1]
        scratch = own + scratch + [pltpu.SemaphoreType.DMA((PARTS + chunks,))]
        out_shape = [pltpu.HBM((r, wide), dtype) for r in (rows, front_rows)]
        out_specs = [hbm, hbm]
    return pl.pallas_call(
        functools.partial(group_kernel, pieces, group, groups, chunks),
        out_shape=tuple(out_shape),
        in_specs=in_specs,
        out_specs=tuple(out_specs),
        scratch_shapes=scratch,
        input_output_aliases=aliases,
        compiler_params=pltpu.CompilerParams(vmem_limit_bytes=SCOPED),
        cost_estimate=pl.CostEstimate(
            flops=2 * count * size * size * width,
            bytes_accessed=(count * size * size + 2 * rows * width) * 2,
            transcendentals=0,
        ),
        name=f"group_{group}",
    )(*operands)


def flush_kernel(count, column, groups, *refs):
    sources, (out_idx, blocks, sides) = refs[:count], refs[count : count + 3]
    width = sources[0].shape[1]
    last = column + 2 == groups
    if last:
        sol_hbm, fsol_hbm, sol, *f_refs, val, more, sems = refs[-5 - count :]
    else:
        sol_hbm, fsol_hbm, sol, *f_refs, val, sems = refs[-4 - count :]
    outs = (sol_hbm, fsol_hbm)
    write, copies = writer(outs, pl.ds(column * width, width), sems)
    row = 0
    for n, ref in enumerate(sources):
        rows = ref.shape[0]
        write(ref, min(n, 1), row, rows)
        row += rows if n else 0

    @pl.when(lax.axis_index("slab") == 0)
    def _():
        cols = pl.ds((column + 1) * width, width)
        to, made = writer(outs, cols, more) if last else (None, [])
        size = blocks.shape[1]
        rows_out, links = out_idx.shape
        later = val.shape[0] // size + rows_out * (links + 1)
        first = blocks.shape[0] // size - later

        def inner(i):
            return sides[pl.ds(i * size, size), cols]

        solve(inner, blocks, first, out_idx, sides, cols, val, sol, f_refs, to)
        for c in made:
            c.wait()

    for c in copies:
        c.wait()


def flushed(sources, out_idx, blocks, sides, outs, column, groups):
    n, dtype = len(sources), sources[0].dtype
    wide = sides.shape[1]
    rows = (sources[0].shape[0], sum(f.shape[0] for f in sources[1:]))
    hbm = pl.BlockSpec(memory_space=pl.ANY)
    vmem = pl.BlockSpec(memory_space=VMEM)
    ins = [*sources, out_idx, blocks, sides]
    held = [pltpu.with_memory_space_constraint(a, VMEM) for a in ins]
    own = [VMEM(a.shape, dtype) for a in sources]
    out_shape = [pltpu.HBM((r, wide), dtype) for r in rows]
    out_specs = [hbm, hbm]
    scratch = [VMEM(sources[0].shape, dtype)]
    if column + 2 == groups:
        scratch = own + scratch + [pltpu.SemaphoreType.DMA((PARTS + n - 1,))]
    else:
        out_shape, out_specs = out_shape + own, out_specs + [vmem] * n
    made = pl.pallas_call(
        functools.partial(flush_kernel, n, column, groups),
        out_shape=tuple(out_shape),
        in_specs=[vmem] * len(ins) + [hbm] * len(outs),
        out_specs=tuple(out_specs),
        scratch_shapes=scratch + [pltpu.SemaphoreType.DMA((n,))],
        input_output_aliases={len(ins) + k: k for k in range(len(outs))},
        compiler_params=pltpu.CompilerParams(vmem_limit_bytes=SCOPED),
        cost_estimate=pl.CostEstimate(
            flops=0,
            bytes_accessed=2 * sum(a.size for a in sources) * dtype.itemsize,
            transcendentals=0,
        ),
        name=f"flush_{column}",
    )(*held, *outs)
    return made[:2], made[2:]


def shards(
    right_sides,
    front_sides,
    pending_front,
    inner_index,
    inner_blocks,
    inner_inverse,
    outer_index,
    outer_blocks,
    front_inverse,
):
    slabs, subs = lax.axis_size("slab"), lax.axis_size("sub")
    columns = pending_front.shape[1]
    groups = right_sides.shape[1] // columns
    in_idx, out_idx = inner_index.T, outer_index
    size = inner_inverse.shape[1]
    weights = (inner_blocks, inner_inverse, outer_blocks, front_inverse)
    blocks, sides, token = staged(
        [w.reshape(-1, size) for w in weights], [right_sides, front_sides]
    )
    arrived, token = gathered(pending_front, slabs, subs, token)
    outs = early = ()
    for group in range(groups):
        made = group_of(
            arrived,
            in_idx,
            out_idx,
            blocks,
            sides,
            outs if group + 1 == groups else early,
            token if group == 0 else None,
            group,
            groups,
        )
        if group + 1 < groups:
            ring = True
            hops = [permuted(f, slabs, subs, 1, 0, ring) for f in made[1:]]
            outs, early = flushed(made, out_idx, blocks, sides, outs, group, groups)
            chunks = []
            for n, hop in enumerate(hops):
                chunk, _ = gathered(hop, slabs, subs)
                chunks.append(chunk)
            arrived = [c[r] for r in range(subs) for c in chunks]
    return tuple(made[:2])


def solution(mesh):
    rows = P(("slab", "sub"), None)
    blocks = P(("slab", "sub"), None, None)
    links = P(("slab", "sub"), None, None, None)
    return jax.shard_map(
        shards,
        mesh=mesh,
        in_specs=(rows, rows, rows, rows, links, blocks, rows, links, blocks),
        out_specs=(rows, rows),
        check_vma=False,
    )
```
